32 devices in a mesh: rows: 16 (over z, y, x), cols: 2 (over core).
Axes of the slice: x: 2, y: 2, z: 4, core: 2. Of those that a mesh axis runs over, the one named last changes fastest.
Arguments:
- panels: float32 [12288, 2, 768], P('rows', None, 'cols'), as said below
- closure_cols: int32 [128, 12], P('rows'), may hold values from -1 to 15, as said below
Outputs:
- factor: float32 [12288, 2, 768], P('rows', None, 'cols')
The draws below stay inside these ranges and needn't reach their ends.
Inputs may be any that keep to these rules, and one draw needn't show every extreme that they name: `closure_cols`: each entry is a block column 0 to 15 of the two supernodes or -1 for an empty slot; entries may repeat; the supernodes' own rows are not read. The block (rows 0 to 767 of panel 0) and the 1536 by 1536 matrix formed by it and rows 768 to 1535 of both panels, mirrored, is symmetric positive definite.
All inputs are finite; a program needn't handle non-finite values.
Results may differ from the reference program's by a relative error of at most 0.000092.
Values sent between devices are 32-bit elements; how exact they have to be, the bound alone decides.
A program may use at most 128 MiB of HBM per device.

```python
import jax
import jax.numpy as jnp
from jax import lax

B = 96
S = 8
K = 12
R = 8
W = 768
NB = 128


def draw_panels(key, part):
    key_rows = jax.random.fold_in(key, 0)
    key_mix = jax.random.fold_in(key, 2)
    key_diag = jax.random.fold_in(key, 3)
    total_rows = NB * B
    below = jax.random.normal(key_rows, (total_rows, 2, W), jnp.float32)
    mixing = jax.random.normal(key_mix, (2 * W, 2 * W), jnp.float32) / jnp.sqrt(2.0 * W)
    dense = jnp.dot(mixing, mixing.T, precision=lax.Precision.HIGHEST)
    dense = 0.5 * (dense + dense.T)
    extra = jnp.exp(jax.random.uniform(key_diag, (2 * W,), jnp.float32, -0.7, 0.7))
    dense = dense + jnp.diag(extra)
    top_rows = jnp.concatenate([dense[:W, :W], jnp.zeros((W, W), jnp.float32)], axis=1).reshape(W, 2, W)
    low_rows = dense[W:, :].reshape(W, 2, W)
    result = below.at[:W].set(top_rows)
    result = result.at[R * B:R * B + W].set(low_rows)
    return result


def draw_closure_cols(key, part):
    key_count, key_vals = jax.random.split(jax.random.fold_in(key, 7), 2)
    counts = jax.random.randint(key_count, (NB, 1), 2 * K // 3, K + 1)
    values = jax.random.randint(key_vals, (NB, K), 0, 2 * S)
    slots = jnp.arange(K)[None, :]
    result = jnp.where(slots < counts, values, -1)
    full_row = values[NB - 1].at[0].set(2 * S - 1)
    result = result.at[NB - 1].set(full_row)
    result = result.at[NB - 2].set(jnp.full((K,), -1, jnp.int32))
    return result.astype(jnp.int32)


def setup_inputs(seed: int = 0) -> dict:
    arg_keys = jax.random.split(jax.random.key(seed), 3)
    return {
        "panels": draw_panels(jax.random.fold_in(arg_keys[2], 71), 0),
        "closure_cols": draw_closure_cols(jax.random.fold_in(arg_keys[2], 71), 0),
    }


def reference(panels, closure_cols):
    rows_total = panels.shape[0]
    block_count = rows_total // B
    block_ids = jnp.arange(block_count)
    column_ids = jnp.arange(2 * S)
    touched = jnp.any(closure_cols[:, :, None] == column_ids[None, None, :], axis=1)
    in_first = block_ids < S
    in_second = (block_ids >= R) & (block_ids < R + S)
    present = jnp.where(in_first[:, None], column_ids[None, :] < S, jnp.where(in_second[:, None], True, touched))
    present = present.astype(jnp.float32)
    kept = panels.reshape(block_count, B, 2, S, B) * present.reshape(block_count, 1, 2, S, 1)
    kept = kept.reshape(rows_total, 2, W)
    first = kept[:, 0, :]
    second = kept[:, 1, :]
    lead_factor = jnp.linalg.cholesky(first[:W])
    panel_one = lax.linalg.triangular_solve(lead_factor, first, left_side=False, lower=True, transpose_a=True)
    lower_left = panel_one[R * B:R * B + W]
    updated = second - jnp.dot(panel_one, lower_left.T, precision=lax.Precision.HIGHEST)
    tail_factor = jnp.linalg.cholesky(updated[R * B:R * B + W])
    panel_two = lax.linalg.triangular_solve(tail_factor, updated, left_side=False, lower=True, transpose_a=True)
    keep_rows = jnp.repeat(1.0 - in_first.astype(jnp.float32), B)
    panel_two = panel_two * keep_rows[:, None]
    return jnp.stack([panel_one, panel_two], axis=1)
```

```python
import functools

import jax
import jax.numpy as jnp
from jax import lax
from jax.experimental import pallas as pl
from jax.experimental.pallas import tpu as pltpu
from jax.sharding import PartitionSpec as P

B = 96
S = 8
R = 8
G = 8
T = 128
NT = (((1,), (1,)), ((), ()))


def broadcast(block, axis, holder):
    block = jnp.where(lax.axis_index(axis) == holder, block, jnp.zeros_like(block))
    return lax.psum(block, axis)


def dot_nt(left, right, precision=lax.Precision.HIGHEST):
    return lax.dot_general(left, right, NT, precision=precision, preferred_element_type=jnp.float32)


def lanes(x, j):
    return jnp.broadcast_to(x[:, j:j + 1], (G, T))


def subs(x, i):
    return jnp.broadcast_to(x[i:i + 1, :], (G, T))


def invert_factor(groups):
    count = T // G
    row = lax.broadcasted_iota(jnp.int32, (G, T), 0)
    col = lax.broadcasted_iota(jnp.int32, (G, T), 1)
    a = list(groups)
    x = [jnp.where(col == row + G * g, 1.0, 0.0).astype(jnp.float32) for g in range(count)]
    out = []
    for p in range(count):
        columns = [lanes(a[p], G * p + k) for k in range(G)]
        s = [[subs(columns[k], i) for k in range(G)] for i in range(G)]
        wa = [subs(a[p], i) for i in range(G)]
        wx = [subs(x[p], i) for i in range(G)]
        fx = list(wx)
        pivots = []
        for k in range(G):
            inv = 1.0 / s[k][k]
            pivots.append(s[k][k])
            scaled = [None] * G
            for j in range(k + 1, G):
                scaled[j] = s[k][j] * inv
            wa[k] = wa[k] * inv
            wx[k] = wx[k] * inv
            low = fx[k] * inv
            for i in range(G):
                if i == k:
                    continue
                for j in range(k + 1, G):
                    s[i][j] = s[i][j] - s[i][k] * scaled[j]
                wa[i] = wa[i] - s[i][k] * wa[k]
                wx[i] = wx[i] - s[i][k] * wx[k]
                if i > k:
                    fx[i] = fx[i] - s[i][k] * low
            for j in range(k + 1, G):
                s[k][j] = scaled[j]
        done = jnp.zeros((G, T), jnp.float32)
        for k in range(G):
            done = jnp.where(row == k, fx[k] * lax.rsqrt(pivots[k]), done)
        out.append(done)
        for g in range(p + 1, count):
            mult = [lanes(a[g], G * p + k) for k in range(G)]
            pa = [mult[k] * wa[k] for k in range(G)]
            px = [mult[k] * wx[k] for k in range(G)]
            while len(pa) > 1:
                pa = [pa[q] + pa[q + 1] for q in range(0, len(pa), 2)]
                px = [px[q] + px[q + 1] for q in range(0, len(px), 2)]
            a[g] = a[g] - pa[0]
            x[g] = x[g] - px[0]
    return out


def factor_kernel(m_ref, x_ref, y_ref, z, t_ref):
    n = m_ref.shape[0]
    extra = x_ref.shape[0]
    total = n + extra
    blocks = n // T
    chunk = 3 * T
    z[:n, :] = m_ref[...]
    z[n:, :] = x_ref[...]

    def step(b, carry):
        here = pl.ds(pl.multiple_of(b * T, T), T)
        block = z[here, here]
        rows = invert_factor([block[G * g:G * (g + 1), :] for g in range(T // G)])
        for g in range(T // G):
            t_ref[G * g:G * (g + 1), :] = rows[g]
        inverse = t_ref[...]

        def scale(c, carry):
            at = pl.ds(pl.multiple_of(c * chunk, chunk), chunk)
            z[at, here] = dot_nt(z[at, here], inverse)
            return carry

        lax.fori_loop((b + 1) // 3, total // chunk, scale, 0)

        def column(j, carry):
            there = pl.ds(pl.multiple_of(j * T, T), T)
            right = z[there, here]

            def update(c, carry):
                at = pl.ds(pl.multiple_of(c * chunk, chunk), chunk)
                z[at, there] = z[at, there] - dot_nt(z[at, here], right)
                return carry

            lax.fori_loop(j // 3, total // chunk, update, 0)
            return carry

        lax.fori_loop(b + 1, blocks, column, 0)
        return carry

    lax.fori_loop(0, blocks, step, 0)
    y_ref[...] = z[n:, :]


def per_device(cols, panels, closure_cols):
    local_rows = panels.shape[0]
    half_width = panels.shape[2]
    width = cols * half_width
    block_count = local_rows // B
    device_row = lax.axis_index("rows")
    core_index = lax.axis_index("cols")
    gathered = lax.all_gather(panels, "cols", axis=2, tiled=True)
    block_ids = device_row * block_count + jnp.arange(block_count)
    column_ids = jnp.arange(2 * S)
    touched = jnp.any(closure_cols[:, :, None] == column_ids[None, None, :], axis=1)
    in_first = block_ids < S
    in_second = (block_ids >= R) & (block_ids < R + S)
    present = jnp.where(
        in_first[:, None], column_ids[None, :] < S, jnp.where(in_second[:, None], True, touched)
    )
    present = present.astype(jnp.float32)
    kept = gathered.reshape(block_count, B, 2, S, B) * present.reshape(block_count, 1, 2, S, 1)
    kept = kept.reshape(local_rows, 2 * width)
    lead = broadcast(kept[:, :width], "rows", 0)
    low = broadcast(kept, "rows", 1)
    matrix = jnp.concatenate(
        [jnp.concatenate([lead, jnp.zeros_like(lead)], axis=1), low], axis=0
    )
    share = local_rows // cols
    mine = lax.dynamic_slice_in_dim(kept, core_index * share, share, 0)
    n = 2 * width
    result = pl.pallas_call(
        factor_kernel,
        out_shape=jax.ShapeDtypeStruct((share, n), jnp.float32),
        in_specs=[pl.BlockSpec(memory_space=pltpu.VMEM)] * 2,
        out_specs=pl.BlockSpec(memory_space=pltpu.VMEM),
        scratch_shapes=[
            pltpu.VMEM((n + share, n), jnp.float32),
            pltpu.VMEM((T, T), jnp.float32),
        ],
        compiler_params=pltpu.CompilerParams(vmem_limit_bytes=48 * 1024 * 1024),
    )(matrix, mine)
    keep_rows = jnp.repeat(1.0 - in_first.astype(jnp.float32), B)
    keep_mine = lax.dynamic_slice_in_dim(keep_rows, core_index * share, share, 0)
    result = result.reshape(share, 2, width)
    result = result * jnp.stack([jnp.ones_like(keep_mine), keep_mine], axis=1)[:, :, None]
    return lax.all_to_all(result, "cols", split_axis=2, concat_axis=0, tiled=True)


def solution(mesh):
    in_specs = (P("rows", None, "cols"), P("rows", None))
    out_specs = P("rows", None, "cols")
    return jax.shard_map(
        functools.partial(per_device, mesh.shape["cols"]),
        mesh=mesh, in_specs=in_specs, out_specs=out_specs, check_vma=False,
    )
```

```python
import functools

import jax
import jax.numpy as jnp
from jax import lax
from jax.experimental import pallas as pl
from jax.experimental.pallas import tpu as pltpu
from jax.sharding import PartitionSpec as P

B = 96
S = 8
R = 8
G = 8
T = 128
NT = (((1,), (1,)), ((), ()))


def dot_nt(left, right, precision=lax.Precision.HIGHEST):
    return lax.dot_general(left, right, NT, precision=precision, preferred_element_type=jnp.float32)


def lanes(x, j):
    return jnp.broadcast_to(x[:, j:j + 1], (G, T))


def subs(x, i):
    return jnp.broadcast_to(x[i:i + 1, :], (G, T))


def invert_factor(groups):
    count = T // G
    row = lax.broadcasted_iota(jnp.int32, (G, T), 0)
    col = lax.broadcasted_iota(jnp.int32, (G, T), 1)
    a = list(groups)
    x = [jnp.where(col == row + G * g, 1.0, 0.0).astype(jnp.float32) for g in range(count)]
    out = []
    for p in range(count):
        columns = [lanes(a[p], G * p + k) for k in range(G)]
        s = [[subs(columns[k], i) for k in range(G)] for i in range(G)]
        wa = [subs(a[p], i) for i in range(G)]
        wx = [subs(x[p], i) for i in range(G)]
        fx = list(wx)
        pivots = []
        for k in range(G):
            inv = 1.0 / s[k][k]
            pivots.append(s[k][k])
            scaled = [None] * G
            for j in range(k + 1, G):
                scaled[j] = s[k][j] * inv
            wa[k] = wa[k] * inv
            wx[k] = wx[k] * inv
            low = fx[k] * inv
            for i in range(G):
                if i == k:
                    continue
                for j in range(k + 1, G):
                    s[i][j] = s[i][j] - s[i][k] * scaled[j]
                wa[i] = wa[i] - s[i][k] * wa[k]
                wx[i] = wx[i] - s[i][k] * wx[k]
                if i > k:
                    fx[i] = fx[i] - s[i][k] * low
            for j in range(k + 1, G):
                s[k][j] = scaled[j]
        done = jnp.zeros((G, T), jnp.float32)
        for k in range(G):
            done = jnp.where(row == k, fx[k] * lax.rsqrt(pivots[k]), done)
        out.append(done)
        for g in range(p + 1, count):
            mult = [lanes(a[g], G * p + k) for k in range(G)]
            pa = [mult[k] * wa[k] for k in range(G)]
            px = [mult[k] * wx[k] for k in range(G)]
            while len(pa) > 1:
                pa = [pa[q] + pa[q + 1] for q in range(0, len(pa), 2)]
                px = [px[q] + px[q + 1] for q in range(0, len(px), 2)]
            a[g] = a[g] - pa[0]
            x[g] = x[g] - px[0]
    return out


def panel_kernel(counts, p_ref, mask_ref, out_ref, z, t_ref, own_send, own_recv, a_recv, b_recv,
                 a_send, b_send, end_send, end_recv):
    rows, cols = counts
    half = p_ref.shape[2]
    local_rows = p_ref.shape[1]
    width = cols * half
    n = 2 * width
    share = local_rows // cols
    per_half = half // T
    blocks = n // T
    chunk = 3 * T
    r = lax.axis_index("rows")
    c = lax.axis_index("cols")
    other = 1 - c
    q, side = r // 2, r % 2
    pairs = rows // 2
    even = q % 2 == 0
    has_near = jnp.logical_and(even, q + 1 < pairs)
    has_far = jnp.logical_and(even, q + 2 < pairs)
    parent = jnp.where(even, r - 4, r - 2)
    across = jnp.where(side == 0, r + 1, r - 1)

    def to(row, core):
        return dict(device_id=(row, core), device_id_type=pl.DeviceIdType.MESH)

    barrier = pltpu.get_barrier_semaphore()
    pl.semaphore_signal(barrier, inc=1, **to(r, other))
    pl.semaphore_signal(barrier, inc=1, **to(across, c))

    @pl.when(q > 0)
    def _():
        pl.semaphore_signal(barrier, inc=1, **to(parent, c))

    heard = 2 + jnp.where(has_near, 1, 0) + jnp.where(has_far, 1, 0)
    pl.semaphore_wait(barrier, heard)

    def place(kind, k, cc):
        column = cc * per_half + k
        if kind == 0:
            return (0, column * T, width - column * T, k * T), (column * T, column * T)
        if k < per_half:
            return (0, 0, width, k * T), (width, column * T)
        k = k - per_half
        column = cc * per_half + k
        return (1, column * T, width - column * T, k * T), (width + column * T, width + column * T)

    def count(kind):
        return per_half if kind == 0 else 2 * per_half

    recvs, sends = (a_recv, b_recv), (a_send, b_send)

    def copy(kind, k, cc, dest, slot, root):
        (panel, first, length, at), (top, left) = place(kind, k, cc)
        there = z.at[pl.ds(top, length), pl.ds(left, T)]
        source = p_ref.at[panel, pl.ds(first, length), pl.ds(at, T)] if root else there
        return pltpu.make_async_remote_copy(
            src_ref=source, dst_ref=there, send_sem=sends[kind].at[slot, k],
            recv_sem=recvs[kind].at[cc, k], **dest)

    def fan_out(kind, k, cc, root):
        @pl.when(has_far)
        def _():
            copy(kind, k, cc, to(r + 4, c), 0, root).start()

        copy(kind, k, cc, to(across, c), 2, root).start()

        @pl.when(has_near)
        def _():
            copy(kind, k, cc, to(r + 2, c), 1, root).start()

        copy(kind, k, cc, to(r, other), 3, root).start()

    def handle(kind, k, cc):
        @pl.when(jnp.logical_and(side == kind, q == 0))
        def _():
            fan_out(kind, k, cc, True)

        @pl.when(jnp.logical_and(side == kind, q > 0))
        def _():
            copy(kind, k, cc, to(r, other), 3, False).wait_recv()
            fan_out(kind, k, cc, False)

        @pl.when(side != kind)
        def _():
            copy(kind, k, cc, to(r, other), 3, False).wait_recv()
            copy(kind, k, cc, to(r, other), 3, False).start()

    def settle(kind, k, cc):
        @pl.when(side == kind)
        def _():
            @pl.when(has_far)
            def _():
                copy(kind, k, cc, to(r, other), 0, False).wait_send()

            @pl.when(has_near)
            def _():
                copy(kind, k, cc, to(r, other), 1, False).wait_send()

            copy(kind, k, cc, to(r, other), 2, False).wait_send()

        copy(kind, k, cc, to(r, other), 3, False).wait_send()
        copy(kind, k, 1 - cc, to(r, other), 3, False).wait_recv()

    def swap(panel):
        return pltpu.make_async_remote_copy(
            src_ref=p_ref.at[panel, pl.ds(pl.multiple_of(other * share, 8), share), :],
            dst_ref=z.at[pl.ds(n, share), pl.ds(pl.multiple_of(panel * width + c * half, T), half)],
            send_sem=own_send.at[panel], recv_sem=own_recv.at[panel], **to(r, other))

    order = []
    for k in range(per_half):
        order += [(0, k), (1, k)]
    order += [(1, k) for k in range(per_half, 2 * per_half)]
    for cc in range(cols):
        @pl.when(c == cc)
        def _():
            for kind, k in order:
                handle(kind, k, cc)

    for panel in range(2):
        swap(panel).start()
        z[pl.ds(n, share), pl.ds(pl.multiple_of(panel * width + c * half, T), half)] = (
            p_ref[panel, pl.ds(pl.multiple_of(c * share, 8), share), :])

    for cc in range(cols):
        @pl.when(c == cc)
        def _():
            for kind in range(2):
                @pl.when(jnp.logical_and(side == kind, q == 0))
                def _():
                    for k in range(count(kind)):
                        (panel, first, length, at), (top, left) = place(kind, k, cc)
                        z[top:top + length, left:left + T] = p_ref[panel, first:first + length, at:at + T]

            for kind, k in order:
                settle(kind, k, cc)

    for panel in range(2):
        swap(panel).wait()
    group = share // B
    for i in range(group):
        at = slice(n + i * B, n + (i + 1) * B)
        z[at, :] = z[at, :] * mask_ref[pl.ds(c * group + i, 1), :]

    def step(b, carry):
        here = pl.ds(pl.multiple_of(b * T, T), T)
        block = z[here, here]
        done = invert_factor([block[G * g:G * (g + 1), :] for g in range(T // G)])
        for g in range(T // G):
            t_ref[G * g:G * (g + 1), :] = done[g]
        inverse = t_ref[...]

        def scale(i, carry):
            at = pl.ds(pl.multiple_of(i * chunk, chunk), chunk)
            z[at, here] = dot_nt(z[at, here], inverse)
            return carry

        lax.fori_loop((b + 1) // 3, (n + share) // chunk, scale, 0)

        def column(j, carry):
            there = pl.ds(pl.multiple_of(j * T, T), T)
            right = z[there, here]

            def update(i, carry):
                at = pl.ds(pl.multiple_of(i * chunk, chunk), chunk)
                z[at, there] = z[at, there] - dot_nt(z[at, here], right)
                return carry

            lax.fori_loop(j // 3, (n + share) // chunk, update, 0)
            return carry

        lax.fori_loop(b + 1, blocks, column, 0)
        return carry

    lax.fori_loop(0, blocks, step, 0)

    for i in range(group):
        at = slice(n + i * B, n + (i + 1) * B)
        keep = jnp.where(r * (local_rows // B) + c * group + i < S, 0.0, 1.0).astype(jnp.float32)
        z[at, width:] = z[at, width:] * keep

    def finish(panel):
        return pltpu.make_async_remote_copy(
            src_ref=z.at[pl.ds(n, share), pl.ds(pl.multiple_of(panel * width + other * half, T), half)],
            dst_ref=out_ref.at[panel, pl.ds(pl.multiple_of(c * share, 8), share), :],
            send_sem=end_send.at[panel], recv_sem=end_recv.at[panel], **to(r, other))

    for panel in range(2):
        finish(panel).start()
        out_ref[panel, pl.ds(pl.multiple_of(c * share, 8), share), :] = (
            z[pl.ds(n, share), pl.ds(pl.multiple_of(panel * width + c * half, T), half)])
    for panel in range(2):
        finish(panel).wait()


def per_device(counts, panels, closure_cols):
    local_rows = panels.shape[0]
    half = panels.shape[2]
    width = counts[1] * half
    n = 2 * width
    share = local_rows // counts[1]
    per_half = half // T
    block_count = local_rows // B
    block_ids = lax.axis_index("rows") * block_count + jnp.arange(block_count)
    column_ids = jnp.arange(2 * S)
    touched = jnp.any(closure_cols[:, :, None] == column_ids[None, None, :], axis=1)
    in_first = block_ids < S
    in_second = (block_ids >= R) & (block_ids < R + S)
    present = jnp.where(
        in_first[:, None], column_ids[None, :] < S, jnp.where(in_second[:, None], True, touched)
    )
    mask = jnp.repeat(present.astype(jnp.float32), B, axis=1)
    dma = pltpu.SemaphoreType.DMA
    result = pl.pallas_call(
        functools.partial(panel_kernel, counts),
        out_shape=jax.ShapeDtypeStruct((2, local_rows, half), jnp.float32),
        in_specs=[pl.BlockSpec(memory_space=pltpu.VMEM)] * 2,
        out_specs=pl.BlockSpec(memory_space=pltpu.VMEM),
        scratch_shapes=[
            pltpu.VMEM((n + share, n), jnp.float32),
            pltpu.VMEM((T, T), jnp.float32),
            dma((2,)), dma((2,)),
            dma((2, per_half)), dma((2, 2 * per_half)),
            dma((4, per_half)), dma((4, 2 * per_half)),
            dma((2,)), dma((2,)),
        ],
        compiler_params=pltpu.CompilerParams(
            vmem_limit_bytes=48 * 1024 * 1024, collective_id=0, has_side_effects=True
        ),
    )(panels.transpose(1, 0, 2), mask)
    return result.transpose(1, 0, 2)


def solution(mesh):
    in_specs = (P("rows", None, "cols"), P("rows", None))
    out_specs = P("rows", None, "cols")
    counts = (mesh.shape["rows"], mesh.shape["cols"])
    return jax.shard_map(
        functools.partial(per_device, counts),
        mesh=mesh, in_specs=in_specs, out_specs=out_specs, check_vma=False,
    )
```

```python
import functools

import jax
import jax.numpy as jnp
from jax import lax
from jax.experimental import pallas as pl
from jax.experimental.pallas import tpu as pltpu
from jax.sharding import PartitionSpec as P

B = 96
S = 8
R = 8
G = 8
T = 128
NT = (((1,), (1,)), ((), ()))


def dot_nt(left, right, precision=lax.Precision.HIGHEST):
    return lax.dot_general(left, right, NT, precision=precision, preferred_element_type=jnp.float32)


def lanes(x, j):
    return jnp.broadcast_to(x[:, j:j + 1], (G, T))


def subs(x, i):
    return jnp.broadcast_to(x[i:i + 1, :], (G, T))


def invert_factor(groups):
    count = T // G
    row = lax.broadcasted_iota(jnp.int32, (G, T), 0)
    col = lax.broadcasted_iota(jnp.int32, (G, T), 1)
    a = list(groups)
    out = []
    for p in range(count):
        columns = [lanes(a[p], G * p + k) for k in range(G)]
        s = {(i, k): subs(columns[k], i) for k in range(G) for i in range(k + 1)}
        here = jnp.logical_and(col >= G * p, col < G * (p + 1))
        unit = jnp.where(col == row + G * p, 1.0, 0.0).astype(jnp.float32)
        start = jnp.where(here, unit, a[p])
        w = [subs(start, i) for i in range(G)]
        inv, m = [], {}
        for k in range(G):
            r = 1.0 / s[k, k]
            inv.append(r)
            for i in range(k + 1, G):
                m[i, k] = s[k, i] * r
            for i in range(k + 1, G):
                for j in range(i, G):
                    s[i, j] = s[i, j] - m[i, k] * s[k, j]
            for i in range(k + 1, G):
                w[i] = w[i] - m[i, k] * w[k]
        done = w[0] * lax.rsqrt(s[0, 0])
        for k in range(1, G):
            done = jnp.where(row == k, w[k] * lax.rsqrt(s[k, k]), done)
        out.append(jnp.where(col < G * (p + 1), done, 0.0))
        if p == count - 1:
            break
        w = [w[k] * inv[k] for k in range(G)]
        for k in range(G - 1, 0, -1):
            for i in range(k):
                w[i] = w[i] - m[k, i] * w[k]
        for g in range(p + 1, count):
            part = [lanes(a[g], G * p + k) * w[k] for k in range(G)]
            while len(part) > 1:
                part = [part[q] + part[q + 1] for q in range(0, len(part), 2)]
            a[g] = jnp.where(here, 0.0, a[g]) - part[0]
    return out


def panel_kernel(counts, p_ref, mask_ref, out_ref, z, t_ref, own_send, own_recv, a_recv, b_recv,
                 a_send, b_send, end_send, end_recv):
    rows, cols = counts
    half = p_ref.shape[2]
    local_rows = p_ref.shape[1]
    width = cols * half
    n = 2 * width
    share = local_rows // cols
    per_half = half // T
    blocks = n // T
    chunk = 3 * T
    r = lax.axis_index("rows")
    c = lax.axis_index("cols")
    other = 1 - c
    q, side = r // 2, r % 2
    pairs = rows // 2
    even = q % 2 == 0
    has_near = jnp.logical_and(even, q + 1 < pairs)
    has_far = jnp.logical_and(even, q + 2 < pairs)
    parent = jnp.where(even, r - 4, r - 2)
    across = jnp.where(side == 0, r + 1, r - 1)

    def to(row, core):
        return dict(device_id=(row, core), device_id_type=pl.DeviceIdType.MESH)

    barrier = pltpu.get_barrier_semaphore()
    pl.semaphore_signal(barrier, inc=1, **to(r, other))
    pl.semaphore_signal(barrier, inc=1, **to(across, c))

    @pl.when(q > 0)
    def _():
        pl.semaphore_signal(barrier, inc=1, **to(parent, c))

    heard = 2 + jnp.where(has_near, 1, 0) + jnp.where(has_far, 1, 0)
    pl.semaphore_wait(barrier, heard)

    def place(kind, k, cc):
        column = cc * per_half + k
        if kind == 0:
            return (0, column * T, width - column * T, k * T), (column * T, column * T)
        if k < per_half:
            return (0, 0, width, k * T), (width, column * T)
        k = k - per_half
        column = cc * per_half + k
        return (1, column * T, width - column * T, k * T), (width + column * T, width + column * T)

    def count(kind):
        return per_half if kind == 0 else 2 * per_half

    recvs, sends = (a_recv, b_recv), (a_send, b_send)

    def copy(kind, k, cc, dest, slot, root):
        (panel, first, length, at), (top, left) = place(kind, k, cc)
        there = z.at[pl.ds(top, length), pl.ds(left, T)]
        source = p_ref.at[panel, pl.ds(first, length), pl.ds(at, T)] if root else there
        return pltpu.make_async_remote_copy(
            src_ref=source, dst_ref=there, send_sem=sends[kind].at[slot, k],
            recv_sem=recvs[kind].at[cc, k], **dest)

    def fan_out(kind, k, cc, root):
        @pl.when(has_far)
        def _():
            copy(kind, k, cc, to(r + 4, c), 0, root).start()

        copy(kind, k, cc, to(across, c), 2, root).start()

        @pl.when(has_near)
        def _():
            copy(kind, k, cc, to(r + 2, c), 1, root).start()

        copy(kind, k, cc, to(r, other), 3, root).start()

    def handle(kind, k, cc):
        @pl.when(jnp.logical_and(side == kind, q == 0))
        def _():
            fan_out(kind, k, cc, True)

        @pl.when(jnp.logical_and(side == kind, q > 0))
        def _():
            copy(kind, k, cc, to(r, other), 3, False).wait_recv()
            fan_out(kind, k, cc, False)

        @pl.when(side != kind)
        def _():
            copy(kind, k, cc, to(r, other), 3, False).wait_recv()
            copy(kind, k, cc, to(r, other), 3, False).start()

    def settle(kind, k, cc):
        @pl.when(side == kind)
        def _():
            @pl.when(has_far)
            def _():
                copy(kind, k, cc, to(r, other), 0, False).wait_send()

            @pl.when(has_near)
            def _():
                copy(kind, k, cc, to(r, other), 1, False).wait_send()

            copy(kind, k, cc, to(r, other), 2, False).wait_send()

        copy(kind, k, cc, to(r, other), 3, False).wait_send()
        copy(kind, k, 1 - cc, to(r, other), 3, False).wait_recv()

    def swap(panel):
        return pltpu.make_async_remote_copy(
            src_ref=p_ref.at[panel, pl.ds(pl.multiple_of(other * share, 8), share), :],
            dst_ref=z.at[pl.ds(n, share), pl.ds(pl.multiple_of(panel * width + c * half, T), half)],
            send_sem=own_send.at[panel], recv_sem=own_recv.at[panel], **to(r, other))

    order = []
    for k in range(per_half):
        order += [(0, k), (1, k)]
    order += [(1, k) for k in range(per_half, 2 * per_half)]
    for cc in range(cols):
        @pl.when(c == cc)
        def _():
            for kind, k in order:
                handle(kind, k, cc)

    for panel in range(2):
        swap(panel).start()
        z[pl.ds(n, share), pl.ds(pl.multiple_of(panel * width + c * half, T), half)] = (
            p_ref[panel, pl.ds(pl.multiple_of(c * share, 8), share), :])

    for cc in range(cols):
        @pl.when(c == cc)
        def _():
            for kind in range(2):
                @pl.when(jnp.logical_and(side == kind, q == 0))
                def _():
                    for k in range(count(kind)):
                        (panel, first, length, at), (top, left) = place(kind, k, cc)
                        z[top:top + length, left:left + T] = p_ref[panel, first:first + length, at:at + T]

            for kind, k in order:
                settle(kind, k, cc)

    for panel in range(2):
        swap(panel).wait()
    group = share // B
    for i in range(group):
        at = slice(n + i * B, n + (i + 1) * B)
        z[at, :] = z[at, :] * mask_ref[pl.ds(c * group + i, 1), :]

    def step(b, carry):
        here = pl.ds(pl.multiple_of(b * T, T), T)
        block = z[here, here]
        done = invert_factor([block[G * g:G * (g + 1), :] for g in range(T // G)])
        for g in range(T // G):
            t_ref[G * g:G * (g + 1), :] = done[g]
        inverse = t_ref[...]

        def scale(i, carry):
            at = pl.ds(pl.multiple_of(i * chunk, chunk), chunk)
            z[at, here] = dot_nt(z[at, here], inverse)
            return carry

        lax.fori_loop((b + 1) // 3, (n + share) // chunk, scale, 0)

        def column(j, carry):
            there = pl.ds(pl.multiple_of(j * 2 * T, 2 * T), 2 * T)
            block_row = j * 2 * T + lax.broadcasted_iota(jnp.int32, (2 * T, T), 0)
            right = jnp.where(block_row >= (b + 1) * T, z[there, here], 0.0)

            def update(i, carry):
                at = pl.ds(pl.multiple_of(i * chunk, chunk), chunk)
                z[at, there] = z[at, there] - dot_nt(z[at, here], right)
                return carry

            lax.fori_loop(2 * j // 3, (n + share) // chunk, update, 0)
            return carry

        lax.fori_loop((b + 1) // 2, blocks // 2, column, 0)
        return carry

    lax.fori_loop(0, blocks, step, 0)

    for i in range(group):
        at = slice(n + i * B, n + (i + 1) * B)
        keep = jnp.where(r * (local_rows // B) + c * group + i < S, 0.0, 1.0).astype(jnp.float32)
        z[at, width:] = z[at, width:] * keep

    def finish(panel):
        return pltpu.make_async_remote_copy(
            src_ref=z.at[pl.ds(n, share), pl.ds(pl.multiple_of(panel * width + other * half, T), half)],
            dst_ref=out_ref.at[panel, pl.ds(pl.multiple_of(c * share, 8), share), :],
            send_sem=end_send.at[panel], recv_sem=end_recv.at[panel], **to(r, other))

    for panel in range(2):
        finish(panel).start()
        out_ref[panel, pl.ds(pl.multiple_of(c * share, 8), share), :] = (
            z[pl.ds(n, share), pl.ds(pl.multiple_of(panel * width + c * half, T), half)])
    for panel in range(2):
        finish(panel).wait()


def per_device(counts, panels, closure_cols):
    local_rows = panels.shape[0]
    half = panels.shape[2]
    width = counts[1] * half
    n = 2 * width
    share = local_rows // counts[1]
    per_half = half // T
    block_count = local_rows // B
    block_ids = lax.axis_index("rows") * block_count + jnp.arange(block_count)
    column_ids = jnp.arange(2 * S)
    touched = jnp.any(closure_cols[:, :, None] == column_ids[None, None, :], axis=1)
    in_first = block_ids < S
    in_second = (block_ids >= R) & (block_ids < R + S)
    present = jnp.where(
        in_first[:, None], column_ids[None, :] < S, jnp.where(in_second[:, None], True, touched)
    )
    mask = jnp.repeat(present.astype(jnp.float32), B, axis=1)
    dma = pltpu.SemaphoreType.DMA
    result = pl.pallas_call(
        functools.partial(panel_kernel, counts),
        out_shape=jax.ShapeDtypeStruct((2, local_rows, half), jnp.float32),
        in_specs=[pl.BlockSpec(memory_space=pltpu.VMEM)] * 2,
        out_specs=pl.BlockSpec(memory_space=pltpu.VMEM),
        scratch_shapes=[
            pltpu.VMEM((n + share, n), jnp.float32),
            pltpu.VMEM((T, T), jnp.float32),
            dma((2,)), dma((2,)),
            dma((2, per_half)), dma((2, 2 * per_half)),
            dma((4, per_half)), dma((4, 2 * per_half)),
            dma((2,)), dma((2,)),
        ],
        compiler_params=pltpu.CompilerParams(
            vmem_limit_bytes=48 * 1024 * 1024, collective_id=0, has_side_effects=True
        ),
    )(panels.transpose(1, 0, 2), mask)
    return result.transpose(1, 0, 2)


def solution(mesh):
    in_specs = (P("rows", None, "cols"), P("rows", None))
    out_specs = P("rows", None, "cols")
    counts = (mesh.shape["rows"], mesh.shape["cols"])
    return jax.shard_map(
        functools.partial(per_device, counts),
        mesh=mesh, in_specs=in_specs, out_specs=out_specs, check_vma=False,
    )
```

```python
import functools

import jax
import jax.numpy as jnp
from jax import lax
from jax.experimental import pallas as pl
from jax.experimental.pallas import tpu as pltpu
from jax.sharding import PartitionSpec as P

B = 96
S = 8
R = 8
G = 8
T = 128
NT = (((1,), (1,)), ((), ()))


def dot_nt(left, right, precision=lax.Precision.HIGHEST):
    return lax.dot_general(left, right, NT, precision=precision, preferred_element_type=jnp.float32)


def lanes(x, j):
    return jnp.broadcast_to(x[:, j:j + 1], (G, T))


def subs(x, i):
    return jnp.broadcast_to(x[i:i + 1, :], (G, T))


def invert_factor(groups, between):
    count = T // G
    row = lax.broadcasted_iota(jnp.int32, (G, T), 0)
    col = lax.broadcasted_iota(jnp.int32, (G, T), 1)
    a = list(groups)
    out = []
    for p in range(count):
        if p in (4, 9, 14):
            between((4, 9, 14).index(p))
        columns = [lanes(a[p], G * p + k) for k in range(G)]
        s = {(i, k): subs(columns[k], i) for k in range(G) for i in range(k + 1)}
        here = jnp.logical_and(col >= G * p, col < G * (p + 1))
        unit = jnp.where(col == row + G * p, 1.0, 0.0).astype(jnp.float32)
        start = jnp.where(here, unit, a[p])
        w = [subs(start, i) for i in range(G)]
        inv, m = [], {}
        for k in range(G):
            r = 1.0 / s[k, k]
            inv.append(r)
            for i in range(k + 1, G):
                m[i, k] = s[k, i] * r
            for i in range(k + 1, G):
                for j in range(i, G):
                    s[i, j] = s[i, j] - m[i, k] * s[k, j]
            for i in range(k + 1, G):
                w[i] = w[i] - m[i, k] * w[k]
        done = w[0] * lax.rsqrt(s[0, 0])
        for k in range(1, G):
            done = jnp.where(row == k, w[k] * lax.rsqrt(s[k, k]), done)
        out.append(jnp.where(col < G * (p + 1), done, 0.0))
        if p == count - 1:
            break
        w = [w[k] * inv[k] for k in range(G)]
        for k in range(G - 1, 0, -1):
            for i in range(k):
                w[i] = w[i] - m[k, i] * w[k]
        for g in range(p + 1, count):
            part = [lanes(a[g], G * p + k) * w[k] for k in range(G)]
            while len(part) > 1:
                part = [part[q] + part[q + 1] for q in range(0, len(part), 2)]
            a[g] = jnp.where(here, 0.0, a[g]) - part[0]
    return out


def panel_kernel(counts, p_ref, mask_ref, out_ref, z, t_ref, own_send, own_recv, a_recv, b_recv,
                 a_send, b_send, end_send, end_recv):
    rows, cols = counts
    half = p_ref.shape[2]
    local_rows = p_ref.shape[1]
    width = cols * half
    n = 2 * width
    share = local_rows // cols
    per_half = half // T
    blocks = n // T
    chunk = 3 * T
    r = lax.axis_index("rows")
    c = lax.axis_index("cols")
    other = 1 - c
    q, side = r // 2, r % 2
    pairs = rows // 2
    even = q % 2 == 0
    has_near = jnp.logical_and(even, q + 1 < pairs)
    has_far = jnp.logical_and(even, q + 2 < pairs)
    parent = jnp.where(even, r - 4, r - 2)
    across = jnp.where(side == 0, r + 1, r - 1)

    def to(row, core):
        return dict(device_id=(row, core), device_id_type=pl.DeviceIdType.MESH)

    barrier = pltpu.get_barrier_semaphore()
    pl.semaphore_signal(barrier, inc=1, **to(r, other))
    pl.semaphore_signal(barrier, inc=1, **to(across, c))

    @pl.when(q > 0)
    def _():
        pl.semaphore_signal(barrier, inc=1, **to(parent, c))

    heard = 2 + jnp.where(has_near, 1, 0) + jnp.where(has_far, 1, 0)
    pl.semaphore_wait(barrier, heard)

    def lead(k, cc, dest, slot, root):
        column = cc * per_half + k
        there = z.at[pl.ds(column * T, width - column * T), pl.ds(column * T, T)]
        near = p_ref.at[0, pl.ds(column * T, width - column * T), pl.ds(k * T, T)]
        return pltpu.make_async_remote_copy(
            src_ref=near if root else there, dst_ref=there, send_sem=a_send.at[slot, k],
            recv_sem=a_recv.at[cc, k], **dest)

    part = width // 2
    pieces = 4 * per_half

    def low(k, core, dest, slot, root):
        panel, column, piece = k // (2 * per_half), (k % (2 * per_half)) // 2, k % 2
        there = z.at[
            pl.ds(pl.multiple_of(width + piece * part, T), part),
            pl.ds(pl.multiple_of(panel * width + core * half + column * T, T), T)]
        near = p_ref.at[
            panel, pl.ds(pl.multiple_of(piece * part, T), part), pl.ds(pl.multiple_of(column * T, T), T)]
        return pltpu.make_async_remote_copy(
            src_ref=near if root else there, dst_ref=there, send_sem=b_send.at[slot, k],
            recv_sem=b_recv.at[core, k], **dest)

    def fan_out(make, k, core, root):
        @pl.when(has_far)
        def _():
            make(k, core, to(r + 4, c), 0, root).start()

        make(k, core, to(across, c), 2, root).start()

        @pl.when(has_near)
        def _():
            make(k, core, to(r + 2, c), 1, root).start()

        make(k, core, to(r, other), 3, root).start()

    def pass_on(make, kind, k, core):
        make(k, core, to(r, other), 3, False).wait_recv()

        @pl.when(side == kind)
        def _():
            fan_out(make, k, core, False)

        @pl.when(side != kind)
        def _():
            make(k, core, to(r, other), 3, False).start()

    def settle(make, kind, k, core, far_core):
        @pl.when(side == kind)
        def _():
            @pl.when(has_far)
            def _():
                make(k, core, to(r, other), 0, False).wait_send()

            @pl.when(has_near)
            def _():
                make(k, core, to(r, other), 1, False).wait_send()

            make(k, core, to(r, other), 2, False).wait_send()

        make(k, core, to(r, other), 3, False).wait_send()
        make(k, far_core, to(r, other), 3, False).wait_recv()

    low_source = jnp.logical_and(side == 1, q == 0)
    lag = (q + 1) // 2 + jnp.where(side == 1, 0, 1)

    def low_turn(t):
        k = t - lag
        mine = jnp.logical_and(k >= 0, k < pieces)
        mine = jnp.logical_and(mine, t < 3 * (blocks // 2))

        @pl.when(jnp.logical_and(jnp.logical_not(low_source), mine))
        def _():
            pass_on(low, 1, k, c)

    def swap(panel):
        return pltpu.make_async_remote_copy(
            src_ref=p_ref.at[panel, pl.ds(pl.multiple_of(other * share, 8), share), :],
            dst_ref=z.at[pl.ds(n, share), pl.ds(pl.multiple_of(panel * width + c * half, T), half)],
            send_sem=own_send.at[panel], recv_sem=own_recv.at[panel], **to(r, other))

    for cc in range(cols):
        @pl.when(c == cc)
        def _():
            @pl.when(jnp.logical_and(side == 0, q == 0))
            def _():
                for k in range(per_half):
                    fan_out(lead, k, cc, True)

            @pl.when(jnp.logical_or(side != 0, q != 0))
            def _():
                for k in range(per_half):
                    pass_on(lead, 0, k, cc)

    @pl.when(low_source)
    def _():
        def send(k, carry):
            fan_out(low, k, c, True)
            return carry

        lax.fori_loop(0, pieces, send, 0)

    for panel in range(2):
        swap(panel).start()
        z[pl.ds(n, share), pl.ds(pl.multiple_of(panel * width + c * half, T), half)] = (
            p_ref[panel, pl.ds(pl.multiple_of(c * share, 8), share), :])

    for cc in range(cols):
        @pl.when(c == cc)
        def _():
            @pl.when(jnp.logical_and(side == 0, q == 0))
            def _():
                z[:width, cc * half:(cc + 1) * half] = p_ref[0]

            for k in range(per_half):
                settle(lead, 0, k, cc, 1 - cc)

    @pl.when(low_source)
    def _():
        for panel in range(2):
            z[width:n, pl.ds(pl.multiple_of(panel * width + c * half, T), half)] = p_ref[panel]

    for panel in range(2):
        swap(panel).wait()
    group = share // B
    for i in range(group):
        at = slice(n + i * B, n + (i + 1) * B)
        z[at, :] = z[at, :] * mask_ref[pl.ds(c * group + i, 1), :]

    lead_chunks, n_chunks, end_chunks = width // chunk, n // chunk, (n + share) // chunk

    def scale_rows(here, inverse, first, last):
        def scale(i, carry):
            at = pl.ds(pl.multiple_of(i * chunk, chunk), chunk)
            z[at, here] = dot_nt(z[at, here], inverse)
            return carry

        lax.fori_loop(first, last, scale, 0)

    def update_rows(b, stop, ranges):
        here = pl.ds(pl.multiple_of(b * T, T), T)

        def column(j, carry):
            there = pl.ds(pl.multiple_of(j * 2 * T, 2 * T), 2 * T)
            block_row = j * 2 * T + lax.broadcasted_iota(jnp.int32, (2 * T, T), 0)
            right = jnp.where(block_row >= (b + 1) * T, z[there, here], 0.0)

            def update(i, carry):
                at = pl.ds(pl.multiple_of(i * chunk, chunk), chunk)
                z[at, there] = z[at, there] - dot_nt(z[at, here], right)
                return carry

            for first, last, lower in ranges:
                begin = jnp.maximum(first, 2 * j // 3) if lower else first
                lax.fori_loop(begin, last, update, 0)
            return carry

        lax.fori_loop((b + 1) // 2, stop, column, 0)

    def panel_step(b, first, last, stop):
        here = pl.ds(pl.multiple_of(b * T, T), T)
        block = z[here, here]

        def between(i):
            low_turn(3 * b + i)

        done = invert_factor([block[G * g:G * (g + 1), :] for g in range(T // G)], between)
        for g in range(T // G):
            t_ref[b, G * g:G * (g + 1), :] = done[g]
        inverse = t_ref[b]
        scale_rows(here, inverse, jnp.maximum(first, (b + 1) // 3), last)
        scale_rows(here, inverse, n_chunks, end_chunks)
        update_rows(b, stop, [(first, last, True), (n_chunks, end_chunks, False)])

    half_blocks = blocks // 2

    def supernode(g, carry):
        @pl.when(g == 1)
        def _():
            @pl.when(jnp.logical_not(low_source))
            def _():
                def rest(k, carry):
                    pass_on(low, 1, k, c)
                    return carry

                lax.fori_loop(jnp.maximum(3 * half_blocks - lag, 0), pieces, rest, 0)

            def settled(k, carry):
                settle(low, 1, k, c, other)
                return carry

            lax.fori_loop(0, pieces, settled, 0)

            def catch_up(b, carry):
                here = pl.ds(pl.multiple_of(b * T, T), T)
                scale_rows(here, t_ref[b], lead_chunks, n_chunks)
                update_rows(b, half_blocks // 2, [(lead_chunks, n_chunks, False)])
                return carry

            lax.fori_loop(0, half_blocks, catch_up, 0)

            def second(j, carry):
                there = pl.ds(pl.multiple_of(width + j * 2 * T, 2 * T), 2 * T)
                right = z[there, :width]

                def update(i, carry):
                    at = pl.ds(pl.multiple_of(i * chunk, chunk), chunk)
                    z[at, there] = z[at, there] - dot_nt(z[at, :width], right)
                    return carry

                lax.fori_loop((width + j * 2 * T) // chunk, end_chunks, update, 0)
                return carry

            lax.fori_loop(0, half_blocks // 2, second, 0)

        def step(i, carry):
            panel_step(
                g * half_blocks + i, g * lead_chunks, (g + 1) * lead_chunks,
                (g + 1) * (half_blocks // 2))
            return carry

        lax.fori_loop(0, half_blocks, step, 0)
        return carry

    lax.fori_loop(0, 2, supernode, 0)

    for i in range(group):
        at = slice(n + i * B, n + (i + 1) * B)
        keep = jnp.where(r * (local_rows // B) + c * group + i < S, 0.0, 1.0).astype(jnp.float32)
        z[at, width:] = z[at, width:] * keep

    def finish(panel):
        return pltpu.make_async_remote_copy(
            src_ref=z.at[pl.ds(n, share), pl.ds(pl.multiple_of(panel * width + other * half, T), half)],
            dst_ref=out_ref.at[panel, pl.ds(pl.multiple_of(c * share, 8), share), :],
            send_sem=end_send.at[panel], recv_sem=end_recv.at[panel], **to(r, other))

    for panel in range(2):
        finish(panel).start()
        out_ref[panel, pl.ds(pl.multiple_of(c * share, 8), share), :] = (
            z[pl.ds(n, share), pl.ds(pl.multiple_of(panel * width + c * half, T), half)])
    for panel in range(2):
        finish(panel).wait()


def per_device(counts, panels, closure_cols):
    local_rows = panels.shape[0]
    half = panels.shape[2]
    width = counts[1] * half
    n = 2 * width
    share = local_rows // counts[1]
    per_half = half // T
    block_count = local_rows // B
    block_ids = lax.axis_index("rows") * block_count + jnp.arange(block_count)
    column_ids = jnp.arange(2 * S)
    touched = jnp.any(closure_cols[:, :, None] == column_ids[None, None, :], axis=1)
    in_first = block_ids < S
    in_second = (block_ids >= R) & (block_ids < R + S)
    present = jnp.where(
        in_first[:, None], column_ids[None, :] < S, jnp.where(in_second[:, None], True, touched)
    )
    mask = jnp.repeat(present.astype(jnp.float32), B, axis=1)
    dma = pltpu.SemaphoreType.DMA
    result = pl.pallas_call(
        functools.partial(panel_kernel, counts),
        out_shape=jax.ShapeDtypeStruct((2, local_rows, half), jnp.float32),
        in_specs=[pl.BlockSpec(memory_space=pltpu.VMEM)] * 2,
        out_specs=pl.BlockSpec(memory_space=pltpu.VMEM),
        scratch_shapes=[
            pltpu.VMEM((n + share, n), jnp.float32),
            pltpu.VMEM((n // T, T, T), jnp.float32),
            dma((2,)), dma((2,)),
            dma((2, per_half)), dma((2, 4 * per_half)),
            dma((4, per_half)), dma((4, 4 * per_half)),
            dma((2,)), dma((2,)),
        ],
        compiler_params=pltpu.CompilerParams(
            vmem_limit_bytes=48 * 1024 * 1024, collective_id=0, has_side_effects=True
        ),
    )(panels.transpose(1, 0, 2), mask)
    return result.transpose(1, 0, 2)


def solution(mesh):
    in_specs = (P("rows", None, "cols"), P("rows", None))
    out_specs = P("rows", None, "cols")
    counts = (mesh.shape["rows"], mesh.shape["cols"])
    return jax.shard_map(
        functools.partial(per_device, counts),
        mesh=mesh, in_specs=in_specs, out_specs=out_specs, check_vma=False,
    )
```

```python
import functools

import jax
import jax.numpy as jnp
from jax import lax
from jax.experimental import pallas as pl
from jax.experimental.pallas import tpu as pltpu
from jax.sharding import PartitionSpec as P

B = 96
S = 8
R = 8
G = 8
T = 128
NT = (((1,), (1,)), ((), ()))


def dot_nt(left, right, precision=lax.Precision.HIGHEST):
    return lax.dot_general(left, right, NT, precision=precision, preferred_element_type=jnp.float32)


def lanes(x, j):
    return jnp.broadcast_to(x[:, j:j + 1], (G, T))


def subs(x, i):
    return jnp.broadcast_to(x[i:i + 1, :], (G, T))


def invert_factor(groups, between):
    count = T // G
    row = lax.broadcasted_iota(jnp.int32, (G, T), 0)
    col = lax.broadcasted_iota(jnp.int32, (G, T), 1)
    a = list(groups)
    out = []
    for p in range(count):
        if p in (4, 9, 14):
            between((4, 9, 14).index(p))
        columns = [lanes(a[p], G * p + k) for k in range(G)]
        s = {(i, k): subs(columns[k], i) for k in range(G) for i in range(k + 1)}
        here = jnp.logical_and(col >= G * p, col < G * (p + 1))
        unit = jnp.where(col == row + G * p, 1.0, 0.0).astype(jnp.float32)
        start = jnp.where(here, unit, a[p])
        e = [lax.rsqrt(s[i, i]) for i in range(G)]
        for i in range(G):
            s[i, i] = 1.0
            for j in range(i + 1, G):
                s[i, j] = s[i, j] * (e[i] * e[j])
        w = [subs(start, i) * e[i] for i in range(G)]
        inv, m = {}, {}
        done = None
        for k in range(0, G, 2):
            first, cross, last = s[k, k], s[k, k + 1], s[k + 1, k + 1]
            det = first * last - cross * cross
            r = 1.0 / det
            inv[k] = (first, cross, last, r)
            for i in range(k + 2, G):
                m[i, k] = (s[k, i] * last - s[k + 1, i] * cross) * r
                m[i, k + 1] = (s[k + 1, i] * first - s[k, i] * cross) * r
            for i in range(k + 2, G):
                for j in range(i, G):
                    s[i, j] = s[i, j] - (m[i, k] * s[k, j] + m[i, k + 1] * s[k + 1, j])
            for i in range(k + 2, G):
                w[i] = w[i] - (m[i, k] * w[k] + m[i, k + 1] * w[k + 1])
        for k in range(0, G, 2):
            first, cross, last, r = inv[k]
            det = first * last - cross * cross
            upper = w[k] if k == 0 else w[k] * lax.rsqrt(first)
            under = (first * w[k + 1] - cross * w[k]) * lax.rsqrt(first * det)
            done = upper if k == 0 else jnp.where(row == k, upper, done)
            done = jnp.where(row == k + 1, under, done)
        out.append(jnp.where(col < G * (p + 1), done, 0.0))
        if p == count - 1:
            break
        v = [None] * G
        for k in range(0, G, 2):
            first, cross, last, r = inv[k]
            v[k] = (last * w[k] - cross * w[k + 1]) * r
            v[k + 1] = (first * w[k + 1] - cross * w[k]) * r
        for k in range(G - 2, 0, -2):
            for i in range(k):
                v[i] = v[i] - (m[k, i] * v[k] + m[k + 1, i] * v[k + 1])
        w = [v[k] * e[k] for k in range(G)]
        for g in range(p + 1, count):
            part = [lanes(a[g], G * p + k) * w[k] for k in range(G)]
            while len(part) > 1:
                part = [part[q] + part[q + 1] for q in range(0, len(part), 2)]
            a[g] = jnp.where(here, 0.0, a[g]) - part[0]
    return out


def panel_kernel(counts, p_ref, mask_ref, out_ref, z, t_ref, own_send, own_recv, a_recv, b_recv,
                 a_send, b_send, end_send, end_recv):
    rows, cols = counts
    half = p_ref.shape[2]
    local_rows = p_ref.shape[1]
    width = cols * half
    n = 2 * width
    share = local_rows // cols
    per_half = half // T
    blocks = n // T
    chunk = 3 * T
    r = lax.axis_index("rows")
    c = lax.axis_index("cols")
    other = 1 - c
    q, side = r // 2, r % 2
    pairs = rows // 2
    even = q % 2 == 0
    has_near = jnp.logical_and(even, q + 1 < pairs)
    has_far = jnp.logical_and(even, q + 2 < pairs)
    parent = jnp.where(even, r - 4, r - 2)
    across = jnp.where(side == 0, r + 1, r - 1)

    def to(row, core):
        return dict(device_id=(row, core), device_id_type=pl.DeviceIdType.MESH)

    barrier = pltpu.get_barrier_semaphore()
    pl.semaphore_signal(barrier, inc=1, **to(r, other))
    pl.semaphore_signal(barrier, inc=1, **to(across, c))

    @pl.when(q > 0)
    def _():
        pl.semaphore_signal(barrier, inc=1, **to(parent, c))

    heard = 2 + jnp.where(has_near, 1, 0) + jnp.where(has_far, 1, 0)
    pl.semaphore_wait(barrier, heard)

    def lead(k, cc, dest, slot, root):
        own, piece = k // 4, k % 4
        column = cc * per_half + own
        length = (width - column * T) // 4
        down = pl.ds(column * T + piece * length, length)
        there = z.at[down, pl.ds(column * T, T)]
        near = p_ref.at[0, down, pl.ds(own * T, T)]
        return pltpu.make_async_remote_copy(
            src_ref=near if root else there, dst_ref=there, send_sem=a_send.at[slot, k],
            recv_sem=a_recv.at[cc, k], **dest)

    part = width // 2
    pieces = 4 * per_half

    def low(k, core, dest, slot, root):
        panel, column, piece = k // (2 * per_half), (k % (2 * per_half)) // 2, k % 2
        there = z.at[
            pl.ds(pl.multiple_of(width + piece * part, T), part),
            pl.ds(pl.multiple_of(panel * width + core * half + column * T, T), T)]
        near = p_ref.at[
            panel, pl.ds(pl.multiple_of(piece * part, T), part), pl.ds(pl.multiple_of(column * T, T), T)]
        return pltpu.make_async_remote_copy(
            src_ref=near if root else there, dst_ref=there, send_sem=b_send.at[slot, k],
            recv_sem=b_recv.at[core, k], **dest)

    def fan_out(make, k, core, root):
        @pl.when(has_far)
        def _():
            make(k, core, to(r + 4, c), 0, root).start()

        make(k, core, to(across, c), 2, root).start()

        @pl.when(has_near)
        def _():
            make(k, core, to(r + 2, c), 1, root).start()

        make(k, core, to(r, other), 3, root).start()

    def pass_on(make, kind, k, core):
        make(k, core, to(r, other), 3, False).wait_recv()

        @pl.when(side == kind)
        def _():
            fan_out(make, k, core, False)

        @pl.when(side != kind)
        def _():
            make(k, core, to(r, other), 3, False).start()

    def settle(make, kind, k, core, far_core):
        @pl.when(side == kind)
        def _():
            @pl.when(has_far)
            def _():
                make(k, core, to(r, other), 0, False).wait_send()

            @pl.when(has_near)
            def _():
                make(k, core, to(r, other), 1, False).wait_send()

            make(k, core, to(r, other), 2, False).wait_send()

        make(k, core, to(r, other), 3, False).wait_send()
        make(k, far_core, to(r, other), 3, False).wait_recv()

    low_source = jnp.logical_and(side == 1, q == 0)
    lag = (q + 1) // 2 + jnp.where(side == 1, 0, 1)

    def low_turn(t):
        k = t - lag
        mine = jnp.logical_and(k >= 0, k < pieces)
        mine = jnp.logical_and(mine, t < 3 * (blocks // 2))

        @pl.when(jnp.logical_and(jnp.logical_not(low_source), mine))
        def _():
            pass_on(low, 1, k, c)

    def swap(panel):
        return pltpu.make_async_remote_copy(
            src_ref=p_ref.at[panel, pl.ds(pl.multiple_of(other * share, 8), share), :],
            dst_ref=z.at[pl.ds(n, share), pl.ds(pl.multiple_of(panel * width + c * half, T), half)],
            send_sem=own_send.at[panel], recv_sem=own_recv.at[panel], **to(r, other))

    for cc in range(cols):
        @pl.when(c == cc)
        def _():
            @pl.when(jnp.logical_and(side == 0, q == 0))
            def _():
                for k in range(4 * per_half):
                    fan_out(lead, k, cc, True)

            @pl.when(jnp.logical_or(side != 0, q != 0))
            def _():
                for k in range(4 * per_half):
                    pass_on(lead, 0, k, cc)

    @pl.when(low_source)
    def _():
        def send(k, carry):
            fan_out(low, k, c, True)
            return carry

        lax.fori_loop(0, pieces, send, 0)

    for panel in range(2):
        swap(panel).start()
        z[pl.ds(n, share), pl.ds(pl.multiple_of(panel * width + c * half, T), half)] = (
            p_ref[panel, pl.ds(pl.multiple_of(c * share, 8), share), :])

    for cc in range(cols):
        @pl.when(c == cc)
        def _():
            @pl.when(jnp.logical_and(side == 0, q == 0))
            def _():
                z[:width, cc * half:(cc + 1) * half] = p_ref[0]

            for k in range(4 * per_half):
                settle(lead, 0, k, cc, 1 - cc)

    @pl.when(low_source)
    def _():
        for panel in range(2):
            z[width:n, pl.ds(pl.multiple_of(panel * width + c * half, T), half)] = p_ref[panel]

    for panel in range(2):
        swap(panel).wait()
    group = share // B
    for i in range(group):
        at = slice(n + i * B, n + (i + 1) * B)
        z[at, :] = z[at, :] * mask_ref[pl.ds(c * group + i, 1), :]

    lead_chunks, n_chunks, end_chunks = width // chunk, n // chunk, (n + share) // chunk

    def scale_rows(here, inverse, first, last):
        def scale(i, carry):
            at = pl.ds(pl.multiple_of(i * chunk, chunk), chunk)
            z[at, here] = dot_nt(z[at, here], inverse)
            return carry

        lax.fori_loop(first, last, scale, 0)

    def update_rows(b, stop, ranges):
        here = pl.ds(pl.multiple_of(b * T, T), T)

        def column(j, carry):
            there = pl.ds(pl.multiple_of(j * 2 * T, 2 * T), 2 * T)
            block_row = j * 2 * T + lax.broadcasted_iota(jnp.int32, (2 * T, T), 0)
            right = jnp.where(block_row >= (b + 1) * T, z[there, here], 0.0)

            def update(i, carry):
                at = pl.ds(pl.multiple_of(i * chunk, chunk), chunk)
                z[at, there] = z[at, there] - dot_nt(z[at, here], right)
                return carry

            for first, last, lower in ranges:
                begin = jnp.maximum(first, 2 * j // 3) if lower else first
                lax.fori_loop(begin, last, update, 0)
            return carry

        lax.fori_loop((b + 1) // 2, stop, column, 0)

    def panel_step(b, first, last, stop):
        here = pl.ds(pl.multiple_of(b * T, T), T)
        block = z[here, here]

        def between(i):
            low_turn(3 * b + i)

        done = invert_factor([block[G * g:G * (g + 1), :] for g in range(T // G)], between)
        for g in range(T // G):
            t_ref[b, G * g:G * (g + 1), :] = done[g]
        inverse = t_ref[b]
        scale_rows(here, inverse, jnp.maximum(first, (b + 1) // 3), last)
        scale_rows(here, inverse, n_chunks, end_chunks)
        update_rows(b, stop, [(first, last, True), (n_chunks, end_chunks, False)])

    half_blocks = blocks // 2

    def supernode(g, carry):
        @pl.when(g == 1)
        def _():
            @pl.when(jnp.logical_not(low_source))
            def _():
                def rest(k, carry):
                    pass_on(low, 1, k, c)
                    return carry

                lax.fori_loop(jnp.maximum(3 * half_blocks - lag, 0), pieces, rest, 0)

            def settled(k, carry):
                settle(low, 1, k, c, other)
                return carry

            lax.fori_loop(0, pieces, settled, 0)

            def catch_up(b, carry):
                here = pl.ds(pl.multiple_of(b * T, T), T)
                scale_rows(here, t_ref[b], lead_chunks, n_chunks)
                update_rows(b, half_blocks // 2, [(lead_chunks, n_chunks, False)])
                return carry

            lax.fori_loop(0, half_blocks, catch_up, 0)

            def second(j, carry):
                there = pl.ds(pl.multiple_of(width + j * 2 * T, 2 * T), 2 * T)
                right = z[there, :width]

                def update(i, carry):
                    at = pl.ds(pl.multiple_of(i * chunk, chunk), chunk)
                    z[at, there] = z[at, there] - dot_nt(z[at, :width], right)
                    return carry

                lax.fori_loop((width + j * 2 * T) // chunk, end_chunks, update, 0)
                return carry

            lax.fori_loop(0, half_blocks // 2, second, 0)

        def step(i, carry):
            panel_step(
                g * half_blocks + i, g * lead_chunks, (g + 1) * lead_chunks,
                (g + 1) * (half_blocks // 2))
            return carry

        lax.fori_loop(0, half_blocks, step, 0)
        return carry

    lax.fori_loop(0, 2, supernode, 0)

    for i in range(group):
        at = slice(n + i * B, n + (i + 1) * B)
        keep = jnp.where(r * (local_rows // B) + c * group + i < S, 0.0, 1.0).astype(jnp.float32)
        z[at, width:] = z[at, width:] * keep

    def finish(panel):
        return pltpu.make_async_remote_copy(
            src_ref=z.at[pl.ds(n, share), pl.ds(pl.multiple_of(panel * width + other * half, T), half)],
            dst_ref=out_ref.at[panel, pl.ds(pl.multiple_of(c * share, 8), share), :],
            send_sem=end_send.at[panel], recv_sem=end_recv.at[panel], **to(r, other))

    for panel in range(2):
        finish(panel).start()
        out_ref[panel, pl.ds(pl.multiple_of(c * share, 8), share), :] = (
            z[pl.ds(n, share), pl.ds(pl.multiple_of(panel * width + c * half, T), half)])
    for panel in range(2):
        finish(panel).wait()


def per_device(counts, panels, closure_cols):
    local_rows = panels.shape[0]
    half = panels.shape[2]
    width = counts[1] * half
    n = 2 * width
    share = local_rows // counts[1]
    per_half = half // T
    block_count = local_rows // B
    block_ids = lax.axis_index("rows") * block_count + jnp.arange(block_count)
    column_ids = jnp.arange(2 * S)
    touched = jnp.any(closure_cols[:, :, None] == column_ids[None, None, :], axis=1)
    in_first = block_ids < S
    in_second = (block_ids >= R) & (block_ids < R + S)
    present = jnp.where(
        in_first[:, None], column_ids[None, :] < S, jnp.where(in_second[:, None], True, touched)
    )
    mask = jnp.repeat(present.astype(jnp.float32), B, axis=1)
    dma = pltpu.SemaphoreType.DMA
    result = pl.pallas_call(
        functools.partial(panel_kernel, counts),
        out_shape=jax.ShapeDtypeStruct((2, local_rows, half), jnp.float32),
        in_specs=[pl.BlockSpec(memory_space=pltpu.VMEM)] * 2,
        out_specs=pl.BlockSpec(memory_space=pltpu.VMEM),
        scratch_shapes=[
            pltpu.VMEM((n + share, n), jnp.float32),
            pltpu.VMEM((n // T, T, T), jnp.float32),
            dma((2,)), dma((2,)),
            dma((2, 4 * per_half)), dma((2, 4 * per_half)),
            dma((4, 4 * per_half)), dma((4, 4 * per_half)),
            dma((2,)), dma((2,)),
        ],
        compiler_params=pltpu.CompilerParams(
            vmem_limit_bytes=48 * 1024 * 1024, collective_id=0, has_side_effects=True
        ),
    )(panels.transpose(1, 0, 2), mask)
    return result.transpose(1, 0, 2)


def solution(mesh):
    in_specs = (P("rows", None, "cols"), P("rows", None))
    out_specs = P("rows", None, "cols")
    counts = (mesh.shape["rows"], mesh.shape["cols"])
    return jax.shard_map(
        functools.partial(per_device, counts),
        mesh=mesh, in_specs=in_specs, out_specs=out_specs, check_vma=False,
    )
```
